32 devices in a mesh: lat: 8 (over z, x), lon: 4 (over y, core).
Axes of the slice: x: 2, y: 2, z: 4, core: 2. Of those that a mesh axis runs over, the one named last changes fastest.
Arguments:
- tangent: float32 [256, 3, 32, 512], P(None, None, 'lat', 'lon'), may hold values from -40 to 40
- base_state: float32 [4, 32, 512], P(None, 'lat', 'lon'), may hold values from -0.4 to 0.8
Outputs:
- fields: float32 [256, 3, 32, 512], P(None, None, 'lat', 'lon')
- upper: float32 [256, 256], replicated
The draws below stay inside these ranges and needn't reach their ends.
All inputs are finite; a program needn't handle non-finite values.
Results may differ from the reference program's by a relative error of at most 0.00012.
Values sent between devices are 32-bit elements; how exact they have to be, the bound alone decides.
A program may use at most 64 MiB of HBM per device.

```python
import math
import jax
import jax.numpy as jnp
from jax import lax

VECS = 256
FIELDS = 3
NLAT = 32
NLON = 512


def draw_tangent(key, part):
    first_key, second_key, third_key = jax.random.split(jax.random.fold_in(key, 11), 3)
    gaussian = jax.random.normal(first_key, (VECS, FIELDS, NLAT, NLON), jnp.float32)
    vector_scale = jnp.exp(jax.random.uniform(second_key, (VECS, 1, 1, 1), jnp.float32, 0.0, math.log(8.0)))
    cell_scale = jnp.exp(jax.random.uniform(third_key, (1, 1, NLAT, NLON), jnp.float32, math.log(0.5), math.log(2.0)))
    values = gaussian * vector_scale * cell_scale
    return jnp.clip(values, -40.0, 40.0)


def draw_base_state(key, part):
    first_key, second_key, third_key = jax.random.split(jax.random.fold_in(key, 23), 3)
    drifts = jax.random.uniform(first_key, (2, NLAT, NLON), jnp.float32, -0.4, 0.4)
    depth_field = jnp.exp(jax.random.uniform(second_key, (1, NLAT, NLON), jnp.float32, math.log(0.2), math.log(0.8)))
    rotation = jax.random.uniform(third_key, (1, NLAT, NLON), jnp.float32, 0.1, 0.5)
    return jnp.concatenate([drifts, depth_field, rotation], axis=0)


def setup_inputs(seed: int = 0) -> dict:
    key_of = jax.random.split(jax.random.key(seed), 3)
    tangent = draw_tangent(jax.random.fold_in(key_of[2], 71), 0)
    base_state = draw_base_state(jax.random.fold_in(key_of[2], 71), 0)
    return dict(tangent=tangent, base_state=base_state)


gravity_coef = 0.5

def east_west(field):
    return 0.5 * (field[..., 1:-1, 2:] - field[..., 1:-1, :-2])

def north_south(field):
    return 0.5 * (field[..., 2:, 1:-1] - field[..., :-2, 1:-1])

def advance(padded, coefficients):
    thickness = padded[:, 0]
    zonal = padded[:, 1]
    meridional = padded[:, 2]
    centre = padded[:, :, 1:-1, 1:-1]
    drift_x = coefficients[0]
    drift_y = coefficients[1]
    depth_field = coefficients[2]
    rotation = coefficients[3]

    def carried(field):
        return drift_x * east_west(field) + drift_y * north_south(field)
    new_thick = centre[:, 0] - carried(thickness) - depth_field * (east_west(zonal) + north_south(meridional))
    new_zonal = centre[:, 1] - carried(zonal) + rotation * centre[:, 2] - gravity_coef * east_west(thickness)
    new_merid = centre[:, 2] - carried(meridional) - rotation * centre[:, 1] - gravity_coef * north_south(thickness)
    return jnp.stack([new_thick, new_zonal, new_merid], axis=1)

def pad_global(state):
    wrapped = jnp.concatenate([state[..., -1:], state, state[..., :1]], axis=-1)
    return jnp.pad(wrapped, ((0, 0), (0, 0), (1, 1), (0, 0)))

def reference(tangent, base_state):
    blocks = tangent.reshape(VECS // 16, 16, FIELDS, NLAT, NLON)

    def evolve(block):
        first = advance(pad_global(block), base_state)
        return advance(pad_global(first), base_state)
    stepped = lax.map(evolve, blocks).reshape(VECS, FIELDS * NLAT * NLON)
    gram = jnp.dot(stepped.astype(jnp.float32), stepped.T.astype(jnp.float32), precision=lax.Precision.HIGHEST, preferred_element_type=jnp.float32) / (NLAT * NLON)
    lower_factor = jnp.linalg.cholesky(gram)
    fields = lax.linalg.triangular_solve(lower_factor, stepped, left_side=True, lower=True)
    return (fields.reshape(VECS, FIELDS, NLAT, NLON), lower_factor.T)
```

```python
import functools

import jax
import jax.numpy as jnp
from jax import lax
from jax.experimental import pallas as pl
from jax.experimental.pallas import tpu as pltpu
from jax.sharding import PartitionSpec as P

MESH = pl.DeviceIdType.MESH
HIGHEST = lax.Precision.HIGHEST
GRAVITY = 0.5
CHUNKS = 4
BLOCK = 32


def dot_t(a, b):
    return lax.dot_general(
        a, b, (((1,), (1,)), ((), ())), precision=HIGHEST, preferred_element_type=jnp.float32
    )


def t_dot(a, b):
    return lax.dot_general(
        a, b, (((0,), (0,)), ((), ())), precision=HIGHEST, preferred_element_type=jnp.float32
    )


def dot(a, b):
    return jnp.dot(a, b, precision=HIGHEST, preferred_element_type=jnp.float32)


def step_kernel(
    lat_n, lon_n, rows, vectors, fused, x_ref, base_ref, s_ref, gram_ref,
    state, above, below, to_west, to_east, from_west, from_east,
    gram, lon_buf, lat_buf, part, piece, gathered,
    row_send, row_recv, col_send, col_recv,
    rs_lon_send, rs_lon_recv, rs_lat_send, rs_lat_recv,
    ag_lat_send, ag_lat_recv, ag_lon_send, ag_lon_recv,
):
    lat = lax.axis_index("lat")
    lon = lax.axis_index("lon")
    cells = x_ref.shape[1]
    size = vectors // CHUNKS
    planes = 3 * rows

    def lon_peer(d):
        return lax.rem(lon + d, lon_n)

    def lat_peer(d):
        return lax.rem(lat + d, lat_n)

    barrier = pltpu.get_barrier_semaphore()
    for d in range(1, lon_n):
        pl.semaphore_signal(barrier, inc=1, device_id=(lat, lon_peer(d)), device_id_type=MESH)
    for d in range(1, lat_n):
        pl.semaphore_signal(barrier, inc=1, device_id=(lat_peer(d), lon), device_id_type=MESH)
    pl.semaphore_wait(barrier, lon_n + lat_n - 2)

    lane = lax.broadcasted_iota(jnp.int32, (size, cells), 1)

    def span(c):
        return pl.ds(c * size, size)

    def row_copy(phase, c, up):
        src = rows - 1 if up else 0
        dst = above if up else below
        side = 0 if up else 1
        peer = lat + 1 if up else lat - 1
        return pltpu.make_async_remote_copy(
            src_ref=state.at[phase, src, :, span(c), :],
            dst_ref=dst.at[phase, :, span(c), :],
            send_sem=row_send.at[phase, c, side],
            recv_sem=row_recv.at[phase, c, side],
            device_id=(peer, lon),
            device_id_type=MESH,
        )

    def col_copy(phase, c, east):
        side = 0 if east else 1
        return pltpu.make_async_remote_copy(
            src_ref=(to_east if east else to_west).at[phase, span(c), :],
            dst_ref=(from_west if east else from_east).at[phase, span(c), :],
            send_sem=col_send.at[phase, c, side],
            recv_sem=col_recv.at[phase, c, side],
            device_id=(lat, lon_peer(1) if east else lon_peer(lon_n - 1)),
            device_id_type=MESH,
        )

    def send(phase, c):
        @pl.when(lat < lat_n - 1)
        def _():
            row_copy(phase, c, True).start()

        @pl.when(lat > 0)
        def _():
            row_copy(phase, c, False).start()

        col_copy(phase, c, True).start()
        col_copy(phase, c, False).start()

    def pack(phase, c):
        west = jnp.zeros((size, cells), jnp.float32)
        east = jnp.zeros((size, cells), jnp.float32)
        for r in range(rows):
            for f in range(3):
                p = f * rows + r
                q = state[phase, r, f, span(c), :]
                west = jnp.where(lane == p, pltpu.roll(q, p, 1) if p else q, west)
                east = jnp.where(lane == p, pltpu.roll(q, p + 1, 1), east)
        to_west[phase, span(c), :] = west
        to_east[phase, span(c), :] = east

    def receive(phase, c):
        @pl.when(lat > 0)
        def _():
            row_copy(phase, c, True).wait_recv()

        @pl.when(lat < lat_n - 1)
        def _():
            row_copy(phase, c, False).wait_recv()

        col_copy(phase, c, True).wait_recv()
        col_copy(phase, c, False).wait_recv()

    def sent(phase, c):
        @pl.when(lat < lat_n - 1)
        def _():
            row_copy(phase, c, True).wait_send()

        @pl.when(lat > 0)
        def _():
            row_copy(phase, c, False).wait_send()

        col_copy(phase, c, True).wait_send()
        col_copy(phase, c, False).wait_send()

    def field(phase, r, f, c):
        if r < 0:
            return above[phase, f, span(c), :]
        if r >= rows:
            return below[phase, f, span(c), :]
        return state[phase, r, f, span(c), :]

    def advance(phase, c):
        west_in = from_west[phase, span(c), :]
        east_in = from_east[phase, span(c), :]

        def across(q, p):
            west = jnp.where(lane == 0, pltpu.roll(west_in, cells - p, 1) if p else west_in, pltpu.roll(q, 1, 1))
            east = jnp.where(lane == cells - 1, pltpu.roll(east_in, cells - 1 - p, 1), pltpu.roll(q, cells - 1, 1))
            return east - west

        for r in range(rows):
            half_x = 0.5 * base_ref[r : r + 1, :]
            half_y = 0.5 * base_ref[rows + r : rows + r + 1, :]
            half_depth = 0.5 * base_ref[2 * rows + r : 2 * rows + r + 1, :]
            rotation = base_ref[3 * rows + r : 3 * rows + r + 1, :]
            h, u, v = (field(phase, r, f, c) for f in range(3))
            hx, ux, vx = (across(q, f * rows + r) for f, q in enumerate((h, u, v)))
            hy, uy, vy = (field(phase, r + 1, f, c) - field(phase, r - 1, f, c) for f in range(3))
            state[phase + 1, r, 0, span(c), :] = h - half_x * hx - half_y * hy - half_depth * (ux + vy)
            state[phase + 1, r, 1, span(c), :] = u - half_x * ux - half_y * uy + rotation * v - (0.5 * GRAVITY) * hx
            state[phase + 1, r, 2, span(c), :] = v - half_x * vx - half_y * vy - rotation * u - (0.5 * GRAVITY) * hy

    @pl.when(lat == 0)
    def _():
        above[...] = jnp.zeros(above.shape, jnp.float32)

    @pl.when(lat == lat_n - 1)
    def _():
        below[...] = jnp.zeros(below.shape, jnp.float32)

    for c in range(CHUNKS):
        for r in range(rows):
            for f in range(3):
                p = f * rows + r
                state[0, r, f, span(c), :] = x_ref[pl.ds(c * size * planes + p, size, stride=planes), :]
        pack(0, c)
        send(0, c)

    for c in range(CHUNKS):
        receive(0, c)
        advance(0, c)
        pack(1, c)
        send(1, c)

    for c in range(CHUNKS):
        receive(1, c)
        advance(1, c)
        high = (c + 1) * size
        total = jnp.zeros((size, high), jnp.float32)
        for r in range(rows):
            for f in range(3):
                s_ref[f * rows + r, span(c), :] = state[2, r, f, span(c), :]
                total += dot_t(state[2, r, f, span(c), :], state[2, r, f, 0:high, :])
        gram[span(c), 0:high] = total

    for phase in range(2):
        for c in range(CHUNKS):
            sent(phase, c)

    for c in range(CHUNKS - 1):
        low = (c + 1) * size
        gram[span(c), low:vectors] = gram[low:vectors, span(c)].T

    if not fused:
        gram_ref[...] = gram[...]
        return

    tall = vectors // lon_n
    short = tall // lat_n

    def rs_lon(d):
        return pltpu.make_async_remote_copy(
            src_ref=gram.at[pl.ds(lon_peer(d) * tall, tall), :],
            dst_ref=lon_buf.at[d - 1],
            send_sem=rs_lon_send.at[d - 1], recv_sem=rs_lon_recv.at[d - 1],
            device_id=(lat, lon_peer(d)), device_id_type=MESH,
        )

    def rs_lat(d):
        return pltpu.make_async_remote_copy(
            src_ref=part.at[pl.ds(lat_peer(d) * short, short), :],
            dst_ref=lat_buf.at[d - 1],
            send_sem=rs_lat_send.at[d - 1], recv_sem=rs_lat_recv.at[d - 1],
            device_id=(lat_peer(d), lon), device_id_type=MESH,
        )

    def ag_lat(d):
        return pltpu.make_async_remote_copy(
            src_ref=piece,
            dst_ref=gathered.at[lat],
            send_sem=ag_lat_send.at[d - 1], recv_sem=ag_lat_recv.at[d - 1],
            device_id=(lat_peer(d), lon), device_id_type=MESH,
        )

    def ag_lon(d):
        return pltpu.make_async_remote_copy(
            src_ref=gathered,
            dst_ref=gram_ref.at[lon],
            send_sem=ag_lon_send.at[d - 1], recv_sem=ag_lon_recv.at[d - 1],
            device_id=(lat, lon_peer(d)), device_id_type=MESH,
        )

    def exchange(copy, n):
        for d in range(1, n):
            copy(d).start()
        for d in range(1, n):
            copy(d).wait()

    exchange(rs_lon, lon_n)
    own = gram[pl.ds(lon * tall, tall), :]
    for d in range(lon_n - 1):
        own += lon_buf[d]
    part[...] = own
    exchange(rs_lat, lat_n)
    own = part[pl.ds(lat * short, short), :]
    for d in range(lat_n - 1):
        own += lat_buf[d]
    piece[...] = own
    gathered[lat] = own
    exchange(ag_lat, lat_n)
    gram_ref[lon] = gathered[...]
    exchange(ag_lon, lon_n)


def factor_kernel(cell_total, g_ref, s_ref, out_ref, upper_ref, work, inverse):
    vectors = g_ref.shape[0]
    planes = s_ref.shape[0]
    cells = s_ref.shape[2]
    size = BLOCK
    lane_count = 2 * size if 2 * size >= 128 else 128
    work[:, 0:vectors] = g_ref[...] * (1.0 / cell_total)
    row_i = lax.broadcasted_iota(jnp.int32, (vectors, vectors), 0)
    col_i = lax.broadcasted_iota(jnp.int32, (vectors, vectors), 1)
    work[:, vectors : 2 * vectors] = jnp.where(row_i == col_i, 1.0, 0.0).astype(jnp.float32)
    t_row = lax.broadcasted_iota(jnp.int32, (size, lane_count), 0)
    t_col = lax.broadcasted_iota(jnp.int32, (size, lane_count), 1)
    unit = jnp.where(t_col == t_row + size, 1.0, 0.0).astype(jnp.float32)
    for b in range(vectors // size):
        lo, hi = b * size, (b + 1) * size
        diag = work[lo:hi, lo:hi]
        tile = jnp.concatenate([diag, jnp.zeros((size, lane_count - size), jnp.float32)], axis=1) + unit
        for k in range(size):
            scale = lax.rsqrt(tile[k : k + 1, k : k + 1])
            pivot = tile[k : k + 1, :] * scale
            mult = jnp.where(t_row > k, tile[:, k : k + 1], 0.0) * scale
            tile = jnp.where(t_row == k, pivot, tile - mult * pivot)
        small = tile[:, size : 2 * size]
        panel = dot(small, work[lo:hi, :])
        u = panel[:, 0:vectors]
        upper_ref[lo:hi, :] = jnp.where(col_i[lo:hi, :] >= row_i[lo:hi, :], u, 0.0)
        inverse[lo:hi, :] = panel[:, vectors : 2 * vectors]
        if hi < vectors:
            work[hi:vectors, :] -= t_dot(panel[:, hi:vectors], panel)
    low = inverse[...]
    for p in range(planes):
        out_ref[pl.ds(p, vectors, stride=planes), :] = dot(low, s_ref[p])


def per_device(tangent, base_state):
    lat_n = lax.axis_size("lat")
    lon_n = lax.axis_size("lon")
    vectors, _, rows, cells = tangent.shape
    planes = 3 * rows
    size = vectors // CHUNKS
    fused = vectors % (lon_n * lat_n * 8) == 0
    tall = vectors // lon_n if fused else 8
    short = tall // lat_n if fused else 8
    f32 = jnp.float32
    x = tangent.reshape(vectors * planes, cells)
    base = base_state.reshape(4 * rows, cells)
    vmem = pl.BlockSpec(memory_space=pltpu.VMEM)
    dma = pltpu.SemaphoreType.DMA
    gram_shape = (lon_n, lat_n, short, vectors) if fused else (vectors, vectors)
    stepped, gram = pl.pallas_call(
        functools.partial(step_kernel, lat_n, lon_n, rows, vectors, fused),
        out_shape=(
            jax.ShapeDtypeStruct((planes, vectors, cells), f32),
            jax.ShapeDtypeStruct(gram_shape, f32),
        ),
        in_specs=[vmem, vmem],
        out_specs=(vmem, vmem),
        scratch_shapes=[
            pltpu.VMEM((3, rows, 3, vectors, cells), f32),
            pltpu.VMEM((2, 3, vectors, cells), f32),
            pltpu.VMEM((2, 3, vectors, cells), f32),
            pltpu.VMEM((2, vectors, cells), f32),
            pltpu.VMEM((2, vectors, cells), f32),
            pltpu.VMEM((2, vectors, cells), f32),
            pltpu.VMEM((2, vectors, cells), f32),
            pltpu.VMEM((vectors, vectors), f32),
            pltpu.VMEM((lon_n - 1, tall, vectors), f32),
            pltpu.VMEM((lat_n - 1, short, vectors), f32),
            pltpu.VMEM((tall, vectors), f32),
            pltpu.VMEM((short, vectors), f32),
            pltpu.VMEM((lat_n, short, vectors), f32),
            dma((2, CHUNKS, 2)), dma((2, CHUNKS, 2)), dma((2, CHUNKS, 2)), dma((2, CHUNKS, 2)),
            dma((lon_n - 1,)), dma((lon_n - 1,)), dma((lat_n - 1,)), dma((lat_n - 1,)),
            dma((lat_n - 1,)), dma((lat_n - 1,)), dma((lon_n - 1,)), dma((lon_n - 1,)),
        ],
        compiler_params=pltpu.CompilerParams(
            collective_id=0, has_side_effects=True, vmem_limit_bytes=40 * 2**20
        ),
    )(x, base)
    if fused:
        gram = gram.reshape(vectors, vectors)
    else:
        gram = lax.psum(gram, ("lat", "lon"))
    cell_total = rows * cells * lat_n * lon_n
    out, upper = pl.pallas_call(
        functools.partial(factor_kernel, cell_total),
        out_shape=(
            jax.ShapeDtypeStruct((vectors * planes, cells), f32),
            jax.ShapeDtypeStruct((vectors, vectors), f32),
        ),
        in_specs=[vmem, vmem],
        out_specs=(vmem, vmem),
        scratch_shapes=[
            pltpu.VMEM((vectors, 2 * vectors), f32),
            pltpu.VMEM((vectors, vectors), f32),
        ],
        compiler_params=pltpu.CompilerParams(vmem_limit_bytes=40 * 2**20),
    )(gram, stepped)
    return out.reshape(tangent.shape), upper


def solution(mesh):
    in_specs = (P(None, None, "lat", "lon"), P(None, "lat", "lon"))
    out_specs = (P(None, None, "lat", "lon"), P())
    return jax.shard_map(
        per_device, mesh=mesh, in_specs=in_specs, out_specs=out_specs, check_vma=False
    )
```

```python
import functools

import jax
import jax.numpy as jnp
from jax import lax
from jax.experimental import pallas as pl
from jax.experimental.pallas import tpu as pltpu
from jax.sharding import PartitionSpec as P

MESH = pl.DeviceIdType.MESH
HIGHEST = lax.Precision.HIGHEST
GRAVITY = 0.5
CHUNKS = 4
BLOCK = 32


def dot_t(a, b):
    return lax.dot_general(
        a, b, (((1,), (1,)), ((), ())), precision=HIGHEST, preferred_element_type=jnp.float32
    )


def t_dot(a, b):
    return lax.dot_general(
        a, b, (((0,), (0,)), ((), ())), precision=HIGHEST, preferred_element_type=jnp.float32
    )


def dot(a, b):
    return jnp.dot(a, b, precision=HIGHEST, preferred_element_type=jnp.float32)


def step_kernel(
    lat_n, lon_n, rows, vectors, fused, x_ref, base_ref, s_ref, gram_ref,
    state, above, below, to_west, to_east, from_west, from_east,
    gram, lon_buf, lat_buf, part, piece, gathered,
    row_send, row_recv, col_send, col_recv,
    rs_lon_send, rs_lon_recv, rs_lat_send, rs_lat_recv,
    ag_lat_send, ag_lat_recv, ag_lon_send, ag_lon_recv,
):
    lat = lax.axis_index("lat")
    lon = lax.axis_index("lon")
    cells = x_ref.shape[1]
    size = vectors // CHUNKS
    planes = 3 * rows

    def lon_peer(d):
        return lax.rem(lon + d, lon_n)

    def lat_peer(d):
        return lax.rem(lat + d, lat_n)

    barrier = pltpu.get_barrier_semaphore()
    for d in range(1, lon_n):
        pl.semaphore_signal(barrier, inc=1, device_id=(lat, lon_peer(d)), device_id_type=MESH)
    for d in range(1, lat_n):
        pl.semaphore_signal(barrier, inc=1, device_id=(lat_peer(d), lon), device_id_type=MESH)
    pl.semaphore_wait(barrier, lon_n + lat_n - 2)

    lane = lax.broadcasted_iota(jnp.int32, (size, cells), 1)

    def span(c):
        return pl.ds(c * size, size)

    def row_copy(phase, c, up):
        src = rows - 1 if up else 0
        dst = above if up else below
        side = 0 if up else 1
        peer = lat + 1 if up else lat - 1
        return pltpu.make_async_remote_copy(
            src_ref=state.at[phase, src, :, span(c), :],
            dst_ref=dst.at[phase, :, span(c), :],
            send_sem=row_send.at[phase, c, side],
            recv_sem=row_recv.at[phase, c, side],
            device_id=(peer, lon),
            device_id_type=MESH,
        )

    def col_copy(phase, c, east):
        side = 0 if east else 1
        return pltpu.make_async_remote_copy(
            src_ref=(to_east if east else to_west).at[phase, span(c), :],
            dst_ref=(from_west if east else from_east).at[phase, span(c), :],
            send_sem=col_send.at[phase, c, side],
            recv_sem=col_recv.at[phase, c, side],
            device_id=(lat, lon_peer(1) if east else lon_peer(lon_n - 1)),
            device_id_type=MESH,
        )

    def send(phase, c):
        @pl.when(lat < lat_n - 1)
        def _():
            row_copy(phase, c, True).start()

        @pl.when(lat > 0)
        def _():
            row_copy(phase, c, False).start()

        col_copy(phase, c, True).start()
        col_copy(phase, c, False).start()

    def pack(phase, c):
        west = jnp.zeros((size, cells), jnp.float32)
        east = jnp.zeros((size, cells), jnp.float32)
        for r in range(rows):
            for f in range(3):
                p = f * rows + r
                q = state[phase, r, f, span(c), :]
                west = jnp.where(lane == p, pltpu.roll(q, p, 1) if p else q, west)
                east = jnp.where(lane == p, pltpu.roll(q, p + 1, 1), east)
        to_west[phase, span(c), :] = west
        to_east[phase, span(c), :] = east

    def receive(phase, c):
        @pl.when(lat > 0)
        def _():
            row_copy(phase, c, True).wait_recv()

        @pl.when(lat < lat_n - 1)
        def _():
            row_copy(phase, c, False).wait_recv()

        col_copy(phase, c, True).wait_recv()
        col_copy(phase, c, False).wait_recv()

    def sent(phase, c):
        @pl.when(lat < lat_n - 1)
        def _():
            row_copy(phase, c, True).wait_send()

        @pl.when(lat > 0)
        def _():
            row_copy(phase, c, False).wait_send()

        col_copy(phase, c, True).wait_send()
        col_copy(phase, c, False).wait_send()

    def field(phase, r, f, c):
        if r < 0:
            return above[phase, f, span(c), :]
        if r >= rows:
            return below[phase, f, span(c), :]
        return state[phase, r, f, span(c), :]

    def advance(phase, c):
        west_in = from_west[phase, span(c), :]
        east_in = from_east[phase, span(c), :]

        def across(q, p):
            west = jnp.where(lane == 0, pltpu.roll(west_in, cells - p, 1) if p else west_in, pltpu.roll(q, 1, 1))
            east = jnp.where(lane == cells - 1, pltpu.roll(east_in, cells - 1 - p, 1), pltpu.roll(q, cells - 1, 1))
            return east - west

        for r in range(rows):
            half_x = 0.5 * base_ref[r : r + 1, :]
            half_y = 0.5 * base_ref[rows + r : rows + r + 1, :]
            half_depth = 0.5 * base_ref[2 * rows + r : 2 * rows + r + 1, :]
            rotation = base_ref[3 * rows + r : 3 * rows + r + 1, :]
            h, u, v = (field(phase, r, f, c) for f in range(3))
            hx, ux, vx = (across(q, f * rows + r) for f, q in enumerate((h, u, v)))
            hy, uy, vy = (field(phase, r + 1, f, c) - field(phase, r - 1, f, c) for f in range(3))
            state[phase + 1, r, 0, span(c), :] = h - half_x * hx - half_y * hy - half_depth * (ux + vy)
            state[phase + 1, r, 1, span(c), :] = u - half_x * ux - half_y * uy + rotation * v - (0.5 * GRAVITY) * hx
            state[phase + 1, r, 2, span(c), :] = v - half_x * vx - half_y * vy - rotation * u - (0.5 * GRAVITY) * hy

    @pl.when(lat == 0)
    def _():
        above[...] = jnp.zeros(above.shape, jnp.float32)

    @pl.when(lat == lat_n - 1)
    def _():
        below[...] = jnp.zeros(below.shape, jnp.float32)

    for c in range(CHUNKS):
        for r in range(rows):
            for f in range(3):
                p = f * rows + r
                state[0, r, f, span(c), :] = x_ref[pl.ds(c * size * planes + p, size, stride=planes), :]
        pack(0, c)
        send(0, c)

    for c in range(CHUNKS):
        receive(0, c)
        advance(0, c)
        pack(1, c)
        send(1, c)

    for c in range(CHUNKS):
        receive(1, c)
        advance(1, c)
        high = (c + 1) * size
        total = jnp.zeros((size, high), jnp.float32)
        for r in range(rows):
            for f in range(3):
                s_ref[f * rows + r, span(c), :] = state[2, r, f, span(c), :]
                total += dot_t(state[2, r, f, span(c), :], state[2, r, f, 0:high, :])
        gram[span(c), 0:high] = total

    for phase in range(2):
        for c in range(CHUNKS):
            sent(phase, c)

    for c in range(CHUNKS - 1):
        low = (c + 1) * size
        gram[span(c), low:vectors] = gram[low:vectors, span(c)].T

    if not fused:
        gram_ref[...] = gram[...]
        return

    tall = vectors // lon_n
    short = tall // lat_n

    def rs_lon(d):
        return pltpu.make_async_remote_copy(
            src_ref=gram.at[pl.ds(lon_peer(d) * tall, tall), :],
            dst_ref=lon_buf.at[d - 1],
            send_sem=rs_lon_send.at[d - 1], recv_sem=rs_lon_recv.at[d - 1],
            device_id=(lat, lon_peer(d)), device_id_type=MESH,
        )

    def rs_lat(d):
        return pltpu.make_async_remote_copy(
            src_ref=part.at[pl.ds(lat_peer(d) * short, short), :],
            dst_ref=lat_buf.at[d - 1],
            send_sem=rs_lat_send.at[d - 1], recv_sem=rs_lat_recv.at[d - 1],
            device_id=(lat_peer(d), lon), device_id_type=MESH,
        )

    def ag_lat(d):
        return pltpu.make_async_remote_copy(
            src_ref=piece,
            dst_ref=gathered.at[lat],
            send_sem=ag_lat_send.at[d - 1], recv_sem=ag_lat_recv.at[d - 1],
            device_id=(lat_peer(d), lon), device_id_type=MESH,
        )

    def ag_lon(d):
        return pltpu.make_async_remote_copy(
            src_ref=gathered,
            dst_ref=gram_ref.at[lon],
            send_sem=ag_lon_send.at[d - 1], recv_sem=ag_lon_recv.at[d - 1],
            device_id=(lat, lon_peer(d)), device_id_type=MESH,
        )

    def exchange(copy, n):
        for d in range(1, n):
            copy(d).start()
        for d in range(1, n):
            copy(d).wait()

    exchange(rs_lon, lon_n)
    own = gram[pl.ds(lon * tall, tall), :]
    for d in range(lon_n - 1):
        own += lon_buf[d]
    part[...] = own
    exchange(rs_lat, lat_n)
    own = part[pl.ds(lat * short, short), :]
    for d in range(lat_n - 1):
        own += lat_buf[d]
    piece[...] = own
    gathered[lat] = own
    exchange(ag_lat, lat_n)
    gram_ref[lon] = gathered[...]
    exchange(ag_lon, lon_n)


def eliminate(tile, size):
    lanes = tile.shape[1]
    row = lax.broadcasted_iota(jnp.int32, (8, lanes), 0)

    def lane(q, k):
        return jnp.broadcast_to(q[:, k : k + 1], (8, lanes))

    def sub(q, k):
        return jnp.broadcast_to(q[k : k + 1, :], (8, lanes))

    groups = [tile[8 * g : 8 * g + 8, :] for g in range(size // 8)]
    for g in range(size // 8):
        cols = [lane(groups[g], 8 * g + j) for j in range(8)]
        below = [[lane(groups[m], 8 * g + j) for j in range(8)] for m in range(g + 1, size // 8)]
        rows = [sub(groups[g], j) for j in range(8)]
        a = {(i, j): sub(cols[j], i) for j in range(8) for i in range(j, 8)}
        scale = []
        for k in range(8):
            scale.append(lax.rsqrt(a[k, k]))
            for i in range(k + 1, 8):
                a[i, k] = a[i, k] * scale[k]
            for j in range(k + 1, 8):
                for i in range(j, 8):
                    a[i, j] = a[i, j] - a[i, k] * a[j, k]
        w = {}
        for i in range(8):
            w[i, i] = scale[i]
            for j in range(i):
                acc = a[i, j] * w[j, j]
                for m in range(j + 1, i):
                    acc = acc + a[i, m] * w[m, j]
                w[i, j] = -acc * scale[i]
        new = None
        for j in range(8):
            column = jnp.zeros((8, lanes), jnp.float32)
            for i in range(j, 8):
                column = jnp.where(row == i, w[i, j], column)
            term = column * rows[j]
            new = term if new is None else new + term
        groups[g] = new
        if g + 1 < size // 8:
            pivots = [sub(new, j) for j in range(8)]
            for n, m in enumerate(range(g + 1, size // 8)):
                change = None
                for j in range(8):
                    mult = None
                    for k in range(j + 1):
                        t = w[j, k] * below[n][k]
                        mult = t if mult is None else mult + t
                    t = mult * pivots[j]
                    change = t if change is None else change + t
                groups[m] = groups[m] - change
    return jnp.concatenate(groups, axis=0)


def factor_kernel(cell_total, g_ref, s_ref, out_ref, upper_ref, work, inverse):
    vectors = g_ref.shape[0]
    planes = s_ref.shape[0]
    cells = s_ref.shape[2]
    size = BLOCK
    lane_count = 2 * size if 2 * size >= 128 else 128
    work[:, 0:vectors] = g_ref[...] * (1.0 / cell_total)
    row_i = lax.broadcasted_iota(jnp.int32, (vectors, vectors), 0)
    col_i = lax.broadcasted_iota(jnp.int32, (vectors, vectors), 1)
    work[:, vectors : 2 * vectors] = jnp.where(row_i == col_i, 1.0, 0.0).astype(jnp.float32)
    t_row = lax.broadcasted_iota(jnp.int32, (size, lane_count), 0)
    t_col = lax.broadcasted_iota(jnp.int32, (size, lane_count), 1)
    unit = jnp.where(t_col == t_row + size, 1.0, 0.0).astype(jnp.float32)
    for b in range(vectors // size):
        lo, hi = b * size, (b + 1) * size
        diag = work[lo:hi, lo:hi]
        tile = jnp.concatenate([diag, jnp.zeros((size, lane_count - size), jnp.float32)], axis=1) + unit
        tile = eliminate(tile, size)
        small = tile[:, size : 2 * size]
        panel = dot(small, work[lo:hi, :])
        u = panel[:, 0:vectors]
        upper_ref[lo:hi, :] = jnp.where(col_i[lo:hi, :] >= row_i[lo:hi, :], u, 0.0)
        inverse[lo:hi, :] = panel[:, vectors : 2 * vectors]
        if hi < vectors:
            work[hi:vectors, :] -= t_dot(panel[:, hi:vectors], panel)
    low = inverse[...]
    for p in range(planes):
        out_ref[pl.ds(p, vectors, stride=planes), :] = dot(low, s_ref[p])


def per_device(tangent, base_state):
    lat_n = lax.axis_size("lat")
    lon_n = lax.axis_size("lon")
    vectors, _, rows, cells = tangent.shape
    planes = 3 * rows
    size = vectors // CHUNKS
    fused = vectors % (lon_n * lat_n * 8) == 0
    tall = vectors // lon_n if fused else 8
    short = tall // lat_n if fused else 8
    f32 = jnp.float32
    x = tangent.reshape(vectors * planes, cells)
    base = base_state.reshape(4 * rows, cells)
    vmem = pl.BlockSpec(memory_space=pltpu.VMEM)
    dma = pltpu.SemaphoreType.DMA
    gram_shape = (lon_n, lat_n, short, vectors) if fused else (vectors, vectors)
    stepped, gram = pl.pallas_call(
        functools.partial(step_kernel, lat_n, lon_n, rows, vectors, fused),
        out_shape=(
            jax.ShapeDtypeStruct((planes, vectors, cells), f32),
            jax.ShapeDtypeStruct(gram_shape, f32),
        ),
        in_specs=[vmem, vmem],
        out_specs=(vmem, vmem),
        scratch_shapes=[
            pltpu.VMEM((3, rows, 3, vectors, cells), f32),
            pltpu.VMEM((2, 3, vectors, cells), f32),
            pltpu.VMEM((2, 3, vectors, cells), f32),
            pltpu.VMEM((2, vectors, cells), f32),
            pltpu.VMEM((2, vectors, cells), f32),
            pltpu.VMEM((2, vectors, cells), f32),
            pltpu.VMEM((2, vectors, cells), f32),
            pltpu.VMEM((vectors, vectors), f32),
            pltpu.VMEM((lon_n - 1, tall, vectors), f32),
            pltpu.VMEM((lat_n - 1, short, vectors), f32),
            pltpu.VMEM((tall, vectors), f32),
            pltpu.VMEM((short, vectors), f32),
            pltpu.VMEM((lat_n, short, vectors), f32),
            dma((2, CHUNKS, 2)), dma((2, CHUNKS, 2)), dma((2, CHUNKS, 2)), dma((2, CHUNKS, 2)),
            dma((lon_n - 1,)), dma((lon_n - 1,)), dma((lat_n - 1,)), dma((lat_n - 1,)),
            dma((lat_n - 1,)), dma((lat_n - 1,)), dma((lon_n - 1,)), dma((lon_n - 1,)),
        ],
        compiler_params=pltpu.CompilerParams(
            collective_id=0, has_side_effects=True, vmem_limit_bytes=40 * 2**20
        ),
    )(x, base)
    if fused:
        gram = gram.reshape(vectors, vectors)
    else:
        gram = lax.psum(gram, ("lat", "lon"))
    cell_total = rows * cells * lat_n * lon_n
    out, upper = pl.pallas_call(
        functools.partial(factor_kernel, cell_total),
        out_shape=(
            jax.ShapeDtypeStruct((vectors * planes, cells), f32),
            jax.ShapeDtypeStruct((vectors, vectors), f32),
        ),
        in_specs=[vmem, vmem],
        out_specs=(vmem, vmem),
        scratch_shapes=[
            pltpu.VMEM((vectors, 2 * vectors), f32),
            pltpu.VMEM((vectors, vectors), f32),
        ],
        compiler_params=pltpu.CompilerParams(vmem_limit_bytes=40 * 2**20),
    )(gram, stepped)
    return out.reshape(tangent.shape), upper


def solution(mesh):
    in_specs = (P(None, None, "lat", "lon"), P(None, "lat", "lon"))
    out_specs = (P(None, None, "lat", "lon"), P())
    return jax.shard_map(
        per_device, mesh=mesh, in_specs=in_specs, out_specs=out_specs, check_vma=False
    )
```

```python
import functools

import jax
import jax.numpy as jnp
from jax import lax
from jax.experimental import pallas as pl
from jax.experimental.pallas import tpu as pltpu
from jax.sharding import PartitionSpec as P

MESH = pl.DeviceIdType.MESH
HIGHEST = lax.Precision.HIGHEST
GRAVITY = 0.5
CHUNKS = 4
BLOCK = 32


def dot_t(a, b):
    return lax.dot_general(
        a, b, (((1,), (1,)), ((), ())), precision=HIGHEST, preferred_element_type=jnp.float32
    )


def t_dot(a, b):
    return lax.dot_general(
        a, b, (((0,), (0,)), ((), ())), precision=HIGHEST, preferred_element_type=jnp.float32
    )


def dot(a, b):
    return jnp.dot(a, b, precision=HIGHEST, preferred_element_type=jnp.float32)


def step_kernel(
    lat_n, lon_n, rows, vectors, fused, x_ref, base_ref, s_ref, first_ref, second_ref,
    state, above, below, to_west, to_east, from_west, from_east,
    gram, lon_buf, lat_buf, whole,
    row_send, row_recv, col_send, col_recv,
    rs_send, rs_recv, lat_send, lat_recv, ag_send, ag_recv,
):
    lat = lax.axis_index("lat")
    lon = lax.axis_index("lon")
    cells = x_ref.shape[1]
    size = vectors // CHUNKS
    planes = 3 * rows

    def lon_peer(d):
        return lax.rem(lon + d, lon_n)

    def lat_peer(d):
        return lax.rem(lat + d, lat_n)

    barrier = pltpu.get_barrier_semaphore()
    for d in range(1, lon_n):
        pl.semaphore_signal(barrier, inc=1, device_id=(lat, lon_peer(d)), device_id_type=MESH)
    for d in range(1, lat_n):
        pl.semaphore_signal(barrier, inc=1, device_id=(lat_peer(d), lon), device_id_type=MESH)
    pl.semaphore_wait(barrier, lon_n + lat_n - 2)

    lane = lax.broadcasted_iota(jnp.int32, (size, cells), 1)

    def span(c):
        return pl.ds(c * size, size)

    def row_copy(phase, c, up):
        src = rows - 1 if up else 0
        dst = above if up else below
        side = 0 if up else 1
        peer = lat + 1 if up else lat - 1
        return pltpu.make_async_remote_copy(
            src_ref=state.at[phase, src, :, span(c), :],
            dst_ref=dst.at[phase, :, span(c), :],
            send_sem=row_send.at[phase, c, side],
            recv_sem=row_recv.at[phase, c, side],
            device_id=(peer, lon),
            device_id_type=MESH,
        )

    def col_copy(phase, c, east):
        side = 0 if east else 1
        return pltpu.make_async_remote_copy(
            src_ref=(to_east if east else to_west).at[phase, span(c), :],
            dst_ref=(from_west if east else from_east).at[phase, span(c), :],
            send_sem=col_send.at[phase, c, side],
            recv_sem=col_recv.at[phase, c, side],
            device_id=(lat, lon_peer(1) if east else lon_peer(lon_n - 1)),
            device_id_type=MESH,
        )

    def send(phase, c):
        @pl.when(lat < lat_n - 1)
        def _():
            row_copy(phase, c, True).start()

        @pl.when(lat > 0)
        def _():
            row_copy(phase, c, False).start()

        col_copy(phase, c, True).start()
        col_copy(phase, c, False).start()

    def pack(phase, c):
        west = jnp.zeros((size, cells), jnp.float32)
        east = jnp.zeros((size, cells), jnp.float32)
        for r in range(rows):
            for f in range(3):
                p = f * rows + r
                q = state[phase, r, f, span(c), :]
                west = jnp.where(lane == p, pltpu.roll(q, p, 1) if p else q, west)
                east = jnp.where(lane == p, pltpu.roll(q, p + 1, 1), east)
        to_west[phase, span(c), :] = west
        to_east[phase, span(c), :] = east

    def receive(phase, c):
        @pl.when(lat > 0)
        def _():
            row_copy(phase, c, True).wait_recv()

        @pl.when(lat < lat_n - 1)
        def _():
            row_copy(phase, c, False).wait_recv()

        col_copy(phase, c, True).wait_recv()
        col_copy(phase, c, False).wait_recv()

    def sent(phase, c):
        @pl.when(lat < lat_n - 1)
        def _():
            row_copy(phase, c, True).wait_send()

        @pl.when(lat > 0)
        def _():
            row_copy(phase, c, False).wait_send()

        col_copy(phase, c, True).wait_send()
        col_copy(phase, c, False).wait_send()

    def field(phase, r, f, c):
        if r < 0:
            return above[phase, f, span(c), :]
        if r >= rows:
            return below[phase, f, span(c), :]
        return state[phase, r, f, span(c), :]

    def advance(phase, c):
        west_in = from_west[phase, span(c), :]
        east_in = from_east[phase, span(c), :]

        def across(q, p):
            west = jnp.where(lane == 0, pltpu.roll(west_in, cells - p, 1) if p else west_in, pltpu.roll(q, 1, 1))
            east = jnp.where(lane == cells - 1, pltpu.roll(east_in, cells - 1 - p, 1), pltpu.roll(q, cells - 1, 1))
            return east - west

        for r in range(rows):
            half_x = 0.5 * base_ref[r : r + 1, :]
            half_y = 0.5 * base_ref[rows + r : rows + r + 1, :]
            half_depth = 0.5 * base_ref[2 * rows + r : 2 * rows + r + 1, :]
            rotation = base_ref[3 * rows + r : 3 * rows + r + 1, :]
            h, u, v = (field(phase, r, f, c) for f in range(3))
            hx, ux, vx = (across(q, f * rows + r) for f, q in enumerate((h, u, v)))
            hy, uy, vy = (field(phase, r + 1, f, c) - field(phase, r - 1, f, c) for f in range(3))
            state[phase + 1, r, 0, span(c), :] = h - half_x * hx - half_y * hy - half_depth * (ux + vy)
            state[phase + 1, r, 1, span(c), :] = u - half_x * ux - half_y * uy + rotation * v - (0.5 * GRAVITY) * hx
            state[phase + 1, r, 2, span(c), :] = v - half_x * vx - half_y * vy - rotation * u - (0.5 * GRAVITY) * hy

    @pl.when(lat == 0)
    def _():
        above[...] = jnp.zeros(above.shape, jnp.float32)

    @pl.when(lat == lat_n - 1)
    def _():
        below[...] = jnp.zeros(below.shape, jnp.float32)

    for c in range(CHUNKS):
        for r in range(rows):
            for f in range(3):
                p = f * rows + r
                state[0, r, f, span(c), :] = x_ref[pl.ds(c * size * planes + p, size, stride=planes), :]
        pack(0, c)
        send(0, c)

    for c in range(CHUNKS):
        receive(0, c)
        advance(0, c)
        pack(1, c)
        send(1, c)

    def gram_rows(c):
        high = (c + 1) * size
        mine, all_so_far = [], []
        for r in range(rows):
            for f in range(3):
                q = state[2, r, f, span(c), :]
                s_ref[f * rows + r, span(c), :] = q
                mine.append(q)
                all_so_far.append(state[2, r, f, 0:high, :])
        gram[span(c), 0:high] = dot_t(
            jnp.concatenate(mine, axis=1), jnp.concatenate(all_so_far, axis=1)
        )

    def halos_sent():
        for phase in range(2):
            for c in range(CHUNKS):
                sent(phase, c)

    if not fused:
        for c in range(CHUNKS):
            receive(1, c)
            advance(1, c)
            gram_rows(c)
        halos_sent()
        for c in range(CHUNKS - 1):
            low = (c + 1) * size
            gram[span(c), low:vectors] = gram[low:vectors, span(c)].T
        first_ref[...] = gram[...]
        second_ref[...] = jnp.zeros(second_ref.shape, jnp.float32)
        return

    inv_ref, low_ref = first_ref, second_ref
    short = size // lon_n
    scale = 1.0 / (rows * cells * lat_n * lon_n)

    def wide(c):
        return -(-((c + 1) * size) // 128) * 128

    def rs(c, d):
        return pltpu.make_async_remote_copy(
            src_ref=gram.at[pl.ds(c * size + lon_peer(d) * short, short), 0 : wide(c)],
            dst_ref=lon_buf.at[c, d - 1, :, 0 : wide(c)],
            send_sem=rs_send.at[c, d - 1], recv_sem=rs_recv.at[c, d - 1],
            device_id=(lat, lon_peer(d)), device_id_type=MESH,
        )

    def over_lat(c, d):
        return pltpu.make_async_remote_copy(
            src_ref=lat_buf.at[c, lat, :, 0 : wide(c)],
            dst_ref=lat_buf.at[c, lat, :, 0 : wide(c)],
            send_sem=lat_send.at[c, d - 1], recv_sem=lat_recv.at[c, d - 1],
            device_id=(lat_peer(d), lon), device_id_type=MESH,
        )

    def ag(c, d):
        return pltpu.make_async_remote_copy(
            src_ref=whole.at[c, lon, :, 0 : wide(c)],
            dst_ref=whole.at[c, lon, :, 0 : wide(c)],
            send_sem=ag_send.at[c, d - 1], recv_sem=ag_recv.at[c, d - 1],
            device_id=(lat, lon_peer(d)), device_id_type=MESH,
        )

    def scatter(c):
        for d in range(1, lon_n):
            rs(c, d).start()

    def across_lat(c):
        for d in range(1, lon_n):
            rs(c, d).wait()
        own = gram[pl.ds(c * size + lon * short, short), 0 : wide(c)]
        for d in range(lon_n - 1):
            own += lon_buf[c, d, :, 0 : wide(c)]
        lat_buf[c, lat, :, 0 : wide(c)] = own
        for d in range(1, lat_n):
            over_lat(c, d).start()

    def gather(c):
        for d in range(1, lat_n):
            over_lat(c, d).wait()
        total = lat_buf[c, 0, :, 0 : wide(c)]
        for i in range(1, lat_n):
            total += lat_buf[c, i, :, 0 : wide(c)]
        whole[c, lon, :, 0 : wide(c)] = total * scale
        for d in range(1, lon_n):
            ag(c, d).start()

    t_row = lax.broadcasted_iota(jnp.int32, (size, 2 * size), 0)
    t_col = lax.broadcasted_iota(jnp.int32, (size, 2 * size), 1)
    unit = jnp.where(t_col == t_row + size, 1.0, 0.0).astype(jnp.float32)
    inv_ref[...] = jnp.zeros(inv_ref.shape, jnp.float32)
    low_ref[...] = jnp.zeros(low_ref.shape, jnp.float32)
    gram[...] = jnp.zeros(gram.shape, jnp.float32)

    def factor(c):
        for d in range(1, lon_n):
            ag(c, d).wait()
        lo, hi = c * size, (c + 1) * size
        mine = whole[c, :, :, 0 : wide(c)].reshape(size, wide(c))
        diag = mine[:, lo:hi]
        if c:
            done = inv_ref[0:lo, 0:lo]
            left = dot_t(mine[:, 0:lo], done)
            diag = diag - dot_t(left, left)
            low_ref[lo:hi, 0:lo] = left
            carry = dot(left, done)
        tile = eliminate(jnp.concatenate([diag, jnp.zeros_like(diag)], axis=1) + unit, size)
        small = tile[:, size : 2 * size]
        inv_ref[lo:hi, lo:hi] = small
        low_ref[lo:hi, lo:hi] = tile[:, 0:size].T
        if c:
            inv_ref[lo:hi, 0:lo] = -dot(small, carry)

    last = CHUNKS - 1
    for c in range(CHUNKS):
        receive(1, c)
        advance(1, c)
        gram_rows(c)
        scatter(c)
        if c >= 1:
            gather(c - 1)
        if c < last:
            across_lat(c)
        if c >= 2:
            factor(c - 2)
    across_lat(last)
    factor(last - 1)
    gather(last)
    factor(last)
    halos_sent()


def eliminate(tile, size):
    lanes = tile.shape[1]
    row = lax.broadcasted_iota(jnp.int32, (8, lanes), 0)

    def lane(q, k):
        return jnp.broadcast_to(q[:, k : k + 1], (8, lanes))

    def sub(q, k):
        return jnp.broadcast_to(q[k : k + 1, :], (8, lanes))

    groups = [tile[8 * g : 8 * g + 8, :] for g in range(size // 8)]
    for g in range(size // 8):
        cols = [lane(groups[g], 8 * g + j) for j in range(8)]
        below = [[lane(groups[m], 8 * g + j) for j in range(8)] for m in range(g + 1, size // 8)]
        rows = [sub(groups[g], j) for j in range(8)]
        a = {(i, j): sub(cols[j], i) for j in range(8) for i in range(j, 8)}
        scale = []
        for k in range(8):
            scale.append(lax.rsqrt(a[k, k]))
            for i in range(k + 1, 8):
                a[i, k] = a[i, k] * scale[k]
            for j in range(k + 1, 8):
                for i in range(j, 8):
                    a[i, j] = a[i, j] - a[i, k] * a[j, k]
        w = {}
        for i in range(8):
            w[i, i] = scale[i]
            for j in range(i):
                acc = a[i, j] * w[j, j]
                for m in range(j + 1, i):
                    acc = acc + a[i, m] * w[m, j]
                w[i, j] = -acc * scale[i]
        new = None
        for j in range(8):
            column = jnp.zeros((8, lanes), jnp.float32)
            for i in range(j, 8):
                column = jnp.where(row == i, w[i, j], column)
            term = column * rows[j]
            new = term if new is None else new + term
        groups[g] = new
        if g + 1 < size // 8:
            pivots = [sub(new, j) for j in range(8)]
            for n, m in enumerate(range(g + 1, size // 8)):
                change = None
                for j in range(8):
                    mult = None
                    for k in range(j + 1):
                        t = w[j, k] * below[n][k]
                        mult = t if mult is None else mult + t
                    t = mult * pivots[j]
                    change = t if change is None else change + t
                groups[m] = groups[m] - change
    return jnp.concatenate(groups, axis=0)


def factor_kernel(cell_total, g_ref, s_ref, out_ref, upper_ref, work, inverse):
    vectors = g_ref.shape[0]
    planes = s_ref.shape[0]
    cells = s_ref.shape[2]
    size = BLOCK
    lane_count = 2 * size if 2 * size >= 128 else 128
    work[:, 0:vectors] = g_ref[...] * (1.0 / cell_total)
    row_i = lax.broadcasted_iota(jnp.int32, (vectors, vectors), 0)
    col_i = lax.broadcasted_iota(jnp.int32, (vectors, vectors), 1)
    work[:, vectors : 2 * vectors] = jnp.where(row_i == col_i, 1.0, 0.0).astype(jnp.float32)
    t_row = lax.broadcasted_iota(jnp.int32, (size, lane_count), 0)
    t_col = lax.broadcasted_iota(jnp.int32, (size, lane_count), 1)
    unit = jnp.where(t_col == t_row + size, 1.0, 0.0).astype(jnp.float32)
    for b in range(vectors // size):
        lo, hi = b * size, (b + 1) * size
        diag = work[lo:hi, lo:hi]
        tile = jnp.concatenate([diag, jnp.zeros((size, lane_count - size), jnp.float32)], axis=1) + unit
        tile = eliminate(tile, size)
        small = tile[:, size : 2 * size]
        panel = dot(small, work[lo:hi, :])
        u = panel[:, 0:vectors]
        upper_ref[lo:hi, :] = jnp.where(col_i[lo:hi, :] >= row_i[lo:hi, :], u, 0.0)
        inverse[lo:hi, :] = panel[:, vectors : 2 * vectors]
        if hi < vectors:
            work[hi:vectors, :] -= t_dot(panel[:, hi:vectors], panel)
    low = inverse[...]
    for p in range(planes):
        out_ref[pl.ds(p, vectors, stride=planes), :] = dot(low, s_ref[p])


def solve_kernel(inv_ref, low_ref, s_ref, out_ref, upper_ref):
    vectors = inv_ref.shape[0]
    planes = s_ref.shape[0]
    cells = s_ref.shape[2]
    row_i = lax.broadcasted_iota(jnp.int32, (vectors, vectors), 0)
    col_i = lax.broadcasted_iota(jnp.int32, (vectors, vectors), 1)
    upper_ref[...] = jnp.where(col_i >= row_i, low_ref[...].T, 0.0)
    low = inv_ref[...]
    for p in range(0, planes, 2):
        both = dot(low, jnp.concatenate([s_ref[p], s_ref[p + 1]], axis=1))
        out_ref[pl.ds(p, vectors, stride=planes), :] = both[:, 0:cells]
        out_ref[pl.ds(p + 1, vectors, stride=planes), :] = both[:, cells : 2 * cells]


def per_device(tangent, base_state):
    lat_n = lax.axis_size("lat")
    lon_n = lax.axis_size("lon")
    vectors, _, rows, cells = tangent.shape
    planes = 3 * rows
    size = vectors // CHUNKS
    fused = size % (lon_n * 8) == 0
    short = size // lon_n if fused else 8
    f32 = jnp.float32
    x = tangent.reshape(vectors * planes, cells)
    base = base_state.reshape(4 * rows, cells)
    vmem = pl.BlockSpec(memory_space=pltpu.VMEM)
    dma = pltpu.SemaphoreType.DMA
    square = jax.ShapeDtypeStruct((vectors, vectors), f32)
    flat = jax.ShapeDtypeStruct((vectors * planes, cells), f32)
    stepped, first, second = pl.pallas_call(
        functools.partial(step_kernel, lat_n, lon_n, rows, vectors, fused),
        out_shape=(jax.ShapeDtypeStruct((planes, vectors, cells), f32), square, square),
        in_specs=[vmem, vmem],
        out_specs=(vmem, vmem, vmem),
        scratch_shapes=[
            pltpu.VMEM((3, rows, 3, vectors, cells), f32),
            pltpu.VMEM((2, 3, vectors, cells), f32),
            pltpu.VMEM((2, 3, vectors, cells), f32),
            pltpu.VMEM((2, vectors, cells), f32),
            pltpu.VMEM((2, vectors, cells), f32),
            pltpu.VMEM((2, vectors, cells), f32),
            pltpu.VMEM((2, vectors, cells), f32),
            pltpu.VMEM((vectors, vectors), f32),
            pltpu.VMEM((CHUNKS, lon_n - 1, short, vectors), f32),
            pltpu.VMEM((CHUNKS, lat_n, short, vectors), f32),
            pltpu.VMEM((CHUNKS, lon_n, short, vectors), f32),
            dma((2, CHUNKS, 2)), dma((2, CHUNKS, 2)), dma((2, CHUNKS, 2)), dma((2, CHUNKS, 2)),
            dma((CHUNKS, lon_n - 1)), dma((CHUNKS, lon_n - 1)),
            dma((CHUNKS, lat_n - 1)), dma((CHUNKS, lat_n - 1)),
            dma((CHUNKS, lon_n - 1)), dma((CHUNKS, lon_n - 1)),
        ],
        compiler_params=pltpu.CompilerParams(
            collective_id=0, has_side_effects=True, vmem_limit_bytes=40 * 2**20
        ),
    )(x, base)
    local = pltpu.CompilerParams(vmem_limit_bytes=40 * 2**20)
    if fused:
        out, upper = pl.pallas_call(
            solve_kernel,
            out_shape=(flat, square),
            in_specs=[vmem, vmem, vmem],
            out_specs=(vmem, vmem),
            compiler_params=local,
        )(first, second, stepped)
    else:
        total = lax.psum(first, ("lat", "lon"))
        cell_total = rows * cells * lat_n * lon_n
        out, upper = pl.pallas_call(
            functools.partial(factor_kernel, cell_total),
            out_shape=(flat, square),
            in_specs=[vmem, vmem],
            out_specs=(vmem, vmem),
            scratch_shapes=[
                pltpu.VMEM((vectors, 2 * vectors), f32),
                pltpu.VMEM((vectors, vectors), f32),
            ],
            compiler_params=local,
        )(total, stepped)
    return out.reshape(tangent.shape), upper


def solution(mesh):
    in_specs = (P(None, None, "lat", "lon"), P(None, "lat", "lon"))
    out_specs = (P(None, None, "lat", "lon"), P())
    return jax.shard_map(
        per_device, mesh=mesh, in_specs=in_specs, out_specs=out_specs, check_vma=False
    )
```

```python
import functools

import jax
import jax.numpy as jnp
from jax import lax
from jax.experimental import pallas as pl
from jax.experimental.pallas import tpu as pltpu
from jax.sharding import PartitionSpec as P

MESH = pl.DeviceIdType.MESH
HIGHEST = lax.Precision.HIGHEST
GRAVITY = 0.5
CHUNKS = 4
BLOCK = 32


def dot_t(a, b):
    return lax.dot_general(
        a, b, (((1,), (1,)), ((), ())), precision=HIGHEST, preferred_element_type=jnp.float32
    )


def t_dot(a, b):
    return lax.dot_general(
        a, b, (((0,), (0,)), ((), ())), precision=HIGHEST, preferred_element_type=jnp.float32
    )


def dot(a, b):
    return jnp.dot(a, b, precision=HIGHEST, preferred_element_type=jnp.float32)


def step_kernel(
    lat_n, lon_n, rows, vectors, fused, x_ref, base_ref, s_ref, first_ref, second_ref,
    state, above, below, to_west, to_east, from_west, from_east,
    gram, lon_buf, lat_buf, whole,
    row_send, row_recv, col_send, col_recv,
    rs_send, rs_recv, lat_send, lat_recv, ag_send, ag_recv,
):
    lat = lax.axis_index("lat")
    lon = lax.axis_index("lon")
    cells = x_ref.shape[1]
    size = vectors // CHUNKS
    planes = 3 * rows

    def lon_peer(d):
        return lax.rem(lon + d, lon_n)

    def lat_peer(d):
        return lax.rem(lat + d, lat_n)

    barrier = pltpu.get_barrier_semaphore()
    for d in range(1, lon_n):
        pl.semaphore_signal(barrier, inc=1, device_id=(lat, lon_peer(d)), device_id_type=MESH)
    for d in range(1, lat_n):
        pl.semaphore_signal(barrier, inc=1, device_id=(lat_peer(d), lon), device_id_type=MESH)
    pl.semaphore_wait(barrier, lon_n + lat_n - 2)

    lane = lax.broadcasted_iota(jnp.int32, (size, cells), 1)

    def span(c):
        return pl.ds(c * size, size)

    def row_copy(phase, c, up):
        src = rows - 1 if up else 0
        dst = above if up else below
        side = 0 if up else 1
        peer = lat + 1 if up else lat - 1
        return pltpu.make_async_remote_copy(
            src_ref=state.at[phase, src, :, span(c), :],
            dst_ref=dst.at[phase, :, span(c), :],
            send_sem=row_send.at[phase, c, side],
            recv_sem=row_recv.at[phase, c, side],
            device_id=(peer, lon),
            device_id_type=MESH,
        )

    def col_copy(phase, c, east):
        side = 0 if east else 1
        return pltpu.make_async_remote_copy(
            src_ref=(to_east if east else to_west).at[phase, span(c), :],
            dst_ref=(from_west if east else from_east).at[phase, span(c), :],
            send_sem=col_send.at[phase, c, side],
            recv_sem=col_recv.at[phase, c, side],
            device_id=(lat, lon_peer(1) if east else lon_peer(lon_n - 1)),
            device_id_type=MESH,
        )

    def send(phase, c):
        @pl.when(lat < lat_n - 1)
        def _():
            row_copy(phase, c, True).start()

        @pl.when(lat > 0)
        def _():
            row_copy(phase, c, False).start()

        col_copy(phase, c, True).start()
        col_copy(phase, c, False).start()

    def pack(phase, c):
        west = jnp.zeros((size, cells), jnp.float32)
        east = jnp.zeros((size, cells), jnp.float32)
        for r in range(rows):
            for f in range(3):
                p = f * rows + r
                q = state[phase, r, f, span(c), :]
                west = jnp.where(lane == p, pltpu.roll(q, p, 1) if p else q, west)
                east = jnp.where(lane == p, pltpu.roll(q, p + 1, 1), east)
        to_west[phase, span(c), :] = west
        to_east[phase, span(c), :] = east

    def receive(phase, c):
        @pl.when(lat > 0)
        def _():
            row_copy(phase, c, True).wait_recv()

        @pl.when(lat < lat_n - 1)
        def _():
            row_copy(phase, c, False).wait_recv()

        col_copy(phase, c, True).wait_recv()
        col_copy(phase, c, False).wait_recv()

    def sent(phase, c):
        @pl.when(lat < lat_n - 1)
        def _():
            row_copy(phase, c, True).wait_send()

        @pl.when(lat > 0)
        def _():
            row_copy(phase, c, False).wait_send()

        col_copy(phase, c, True).wait_send()
        col_copy(phase, c, False).wait_send()

    def field(phase, r, f, c):
        if r < 0:
            return above[phase, f, span(c), :]
        if r >= rows:
            return below[phase, f, span(c), :]
        return state[phase, r, f, span(c), :]

    def advance(phase, c):
        west_in = from_west[phase, span(c), :]
        east_in = from_east[phase, span(c), :]

        def across(q, p):
            west = jnp.where(lane == 0, pltpu.roll(west_in, cells - p, 1) if p else west_in, pltpu.roll(q, 1, 1))
            east = jnp.where(lane == cells - 1, pltpu.roll(east_in, cells - 1 - p, 1), pltpu.roll(q, cells - 1, 1))
            return east - west

        for r in range(rows):
            half_x = 0.5 * base_ref[r : r + 1, :]
            half_y = 0.5 * base_ref[rows + r : rows + r + 1, :]
            half_depth = 0.5 * base_ref[2 * rows + r : 2 * rows + r + 1, :]
            rotation = base_ref[3 * rows + r : 3 * rows + r + 1, :]
            h, u, v = (field(phase, r, f, c) for f in range(3))
            hx, ux, vx = (across(q, f * rows + r) for f, q in enumerate((h, u, v)))
            hy, uy, vy = (field(phase, r + 1, f, c) - field(phase, r - 1, f, c) for f in range(3))
            state[phase + 1, r, 0, span(c), :] = h - half_x * hx - half_y * hy - half_depth * (ux + vy)
            state[phase + 1, r, 1, span(c), :] = u - half_x * ux - half_y * uy + rotation * v - (0.5 * GRAVITY) * hx
            state[phase + 1, r, 2, span(c), :] = v - half_x * vx - half_y * vy - rotation * u - (0.5 * GRAVITY) * hy

    @pl.when(lat == 0)
    def _():
        above[...] = jnp.zeros(above.shape, jnp.float32)

    @pl.when(lat == lat_n - 1)
    def _():
        below[...] = jnp.zeros(below.shape, jnp.float32)

    def begin(c):
        for r in range(rows):
            for f in range(3):
                p = f * rows + r
                state[0, r, f, span(c), :] = x_ref[pl.ds(c * size * planes + p, size, stride=planes), :]
        pack(0, c)
        send(0, c)

    def middle(c):
        receive(0, c)
        advance(0, c)
        pack(1, c)
        send(1, c)

    def halos(c):
        if c == 0:
            begin(0)
            begin(1)
            sent(0, 0)
            begin(2)
            middle(0)
            sent(0, 1)
            for n in range(3, CHUNKS):
                begin(n)
            middle(1)
        if c + 2 < CHUNKS:
            middle(c + 2)
        receive(1, c)
        advance(1, c)

    def gram_rows(c):
        high = (c + 1) * size
        mine, all_so_far = [], []
        for r in range(rows):
            for f in range(3):
                q = state[2, r, f, span(c), :]
                s_ref[f * rows + r, span(c), :] = q
                mine.append(q)
                all_so_far.append(state[2, r, f, 0:high, :])
        gram[span(c), 0:high] = dot_t(
            jnp.concatenate(mine, axis=1), jnp.concatenate(all_so_far, axis=1)
        )

    def halos_sent():
        for c in range(2, CHUNKS):
            sent(0, c)
        for c in range(CHUNKS):
            sent(1, c)

    if not fused:
        for c in range(CHUNKS):
            halos(c)
            gram_rows(c)
        halos_sent()
        for c in range(CHUNKS - 1):
            low = (c + 1) * size
            gram[span(c), low:vectors] = gram[low:vectors, span(c)].T
        first_ref[...] = gram[...]
        second_ref[...] = jnp.zeros(second_ref.shape, jnp.float32)
        return

    inv_ref, low_ref = first_ref, second_ref
    short = size // lon_n
    scale = 1.0 / (rows * cells * lat_n * lon_n)

    def wide(c):
        return -(-((c + 1) * size) // 128) * 128

    def rs(c, d):
        return pltpu.make_async_remote_copy(
            src_ref=gram.at[pl.ds(c * size + lon_peer(d) * short, short), 0 : wide(c)],
            dst_ref=lon_buf.at[c, d - 1, :, 0 : wide(c)],
            send_sem=rs_send.at[c, d - 1], recv_sem=rs_recv.at[c, d - 1],
            device_id=(lat, lon_peer(d)), device_id_type=MESH,
        )

    def over_lat(c, d):
        return pltpu.make_async_remote_copy(
            src_ref=lat_buf.at[c, lat, :, 0 : wide(c)],
            dst_ref=lat_buf.at[c, lat, :, 0 : wide(c)],
            send_sem=lat_send.at[c, d - 1], recv_sem=lat_recv.at[c, d - 1],
            device_id=(lat_peer(d), lon), device_id_type=MESH,
        )

    def ag(c, d):
        return pltpu.make_async_remote_copy(
            src_ref=whole.at[c, lon, :, 0 : wide(c)],
            dst_ref=whole.at[c, lon, :, 0 : wide(c)],
            send_sem=ag_send.at[c, d - 1], recv_sem=ag_recv.at[c, d - 1],
            device_id=(lat, lon_peer(d)), device_id_type=MESH,
        )

    def scatter(c):
        for d in range(1, lon_n):
            rs(c, d).start()

    def across_lat(c):
        for d in range(1, lon_n):
            rs(c, d).wait()
        own = gram[pl.ds(c * size + lon * short, short), 0 : wide(c)]
        for d in range(lon_n - 1):
            own += lon_buf[c, d, :, 0 : wide(c)]
        lat_buf[c, lat, :, 0 : wide(c)] = own
        for d in range(1, lat_n):
            over_lat(c, d).start()

    def gather(c):
        for d in range(1, lat_n):
            over_lat(c, d).wait()
        total = lat_buf[c, 0, :, 0 : wide(c)]
        for i in range(1, lat_n):
            total += lat_buf[c, i, :, 0 : wide(c)]
        whole[c, lon, :, 0 : wide(c)] = total * scale
        for d in range(1, lon_n):
            ag(c, d).start()

    t_row = lax.broadcasted_iota(jnp.int32, (size, 2 * size), 0)
    t_col = lax.broadcasted_iota(jnp.int32, (size, 2 * size), 1)
    unit = jnp.where(t_col == t_row + size, 1.0, 0.0).astype(jnp.float32)
    inv_ref[...] = jnp.zeros(inv_ref.shape, jnp.float32)
    low_ref[...] = jnp.zeros(low_ref.shape, jnp.float32)
    gram[...] = jnp.zeros(gram.shape, jnp.float32)

    def factor(c):
        for d in range(1, lon_n):
            ag(c, d).wait()
        lo, hi = c * size, (c + 1) * size
        mine = whole[c, :, :, 0 : wide(c)].reshape(size, wide(c))
        diag = mine[:, lo:hi]
        if c:
            done = inv_ref[0:lo, 0:lo]
            left = dot_t(mine[:, 0:lo], done)
            diag = diag - dot_t(left, left)
            low_ref[lo:hi, 0:lo] = left
            carry = dot(left, done)
        tile = eliminate(jnp.concatenate([diag, jnp.zeros_like(diag)], axis=1) + unit, size)
        small = tile[:, size : 2 * size]
        inv_ref[lo:hi, lo:hi] = small
        low_ref[lo:hi, lo:hi] = tile[:, 0:size].T
        if c:
            inv_ref[lo:hi, 0:lo] = -dot(small, carry)

    last = CHUNKS - 1
    for c in range(CHUNKS):
        halos(c)
        gram_rows(c)
        scatter(c)
        if c >= 1:
            gather(c - 1)
        if c < last:
            across_lat(c)
        if c >= 2:
            factor(c - 2)
    across_lat(last)
    factor(last - 1)
    gather(last)
    factor(last)
    halos_sent()


def eliminate(tile, size):
    lanes = tile.shape[1]
    row = lax.broadcasted_iota(jnp.int32, (8, lanes), 0)

    def lane(q, k):
        return jnp.broadcast_to(q[:, k : k + 1], (8, lanes))

    def sub(q, k):
        return jnp.broadcast_to(q[k : k + 1, :], (8, lanes))

    groups = [tile[8 * g : 8 * g + 8, :] for g in range(size // 8)]
    for g in range(size // 8):
        cols = [lane(groups[g], 8 * g + j) for j in range(8)]
        below = [[lane(groups[m], 8 * g + j) for j in range(8)] for m in range(g + 1, size // 8)]
        rows = [sub(groups[g], j) for j in range(8)]
        a = {(i, j): sub(cols[j], i) for j in range(8) for i in range(j, 8)}
        scale = []
        for k in range(8):
            scale.append(lax.rsqrt(a[k, k]))
            for i in range(k + 1, 8):
                a[i, k] = a[i, k] * scale[k]
            for j in range(k + 1, 8):
                for i in range(j, 8):
                    a[i, j] = a[i, j] - a[i, k] * a[j, k]
        w = {}
        for i in range(8):
            w[i, i] = scale[i]
            for j in range(i):
                acc = a[i, j] * w[j, j]
                for m in range(j + 1, i):
                    acc = acc + a[i, m] * w[m, j]
                w[i, j] = -acc * scale[i]
        new = None
        for j in range(8):
            column = jnp.zeros((8, lanes), jnp.float32)
            for i in range(j, 8):
                column = jnp.where(row == i, w[i, j], column)
            term = column * rows[j]
            new = term if new is None else new + term
        groups[g] = new
        if g + 1 < size // 8:
            pivots = [sub(new, j) for j in range(8)]
            for n, m in enumerate(range(g + 1, size // 8)):
                change = None
                for j in range(8):
                    mult = None
                    for k in range(j + 1):
                        t = w[j, k] * below[n][k]
                        mult = t if mult is None else mult + t
                    t = mult * pivots[j]
                    change = t if change is None else change + t
                groups[m] = groups[m] - change
    return jnp.concatenate(groups, axis=0)


def factor_kernel(cell_total, g_ref, s_ref, out_ref, upper_ref, work, inverse):
    vectors = g_ref.shape[0]
    planes = s_ref.shape[0]
    cells = s_ref.shape[2]
    size = BLOCK
    lane_count = 2 * size if 2 * size >= 128 else 128
    work[:, 0:vectors] = g_ref[...] * (1.0 / cell_total)
    row_i = lax.broadcasted_iota(jnp.int32, (vectors, vectors), 0)
    col_i = lax.broadcasted_iota(jnp.int32, (vectors, vectors), 1)
    work[:, vectors : 2 * vectors] = jnp.where(row_i == col_i, 1.0, 0.0).astype(jnp.float32)
    t_row = lax.broadcasted_iota(jnp.int32, (size, lane_count), 0)
    t_col = lax.broadcasted_iota(jnp.int32, (size, lane_count), 1)
    unit = jnp.where(t_col == t_row + size, 1.0, 0.0).astype(jnp.float32)
    for b in range(vectors // size):
        lo, hi = b * size, (b + 1) * size
        diag = work[lo:hi, lo:hi]
        tile = jnp.concatenate([diag, jnp.zeros((size, lane_count - size), jnp.float32)], axis=1) + unit
        tile = eliminate(tile, size)
        small = tile[:, size : 2 * size]
        panel = dot(small, work[lo:hi, :])
        u = panel[:, 0:vectors]
        upper_ref[lo:hi, :] = jnp.where(col_i[lo:hi, :] >= row_i[lo:hi, :], u, 0.0)
        inverse[lo:hi, :] = panel[:, vectors : 2 * vectors]
        if hi < vectors:
            work[hi:vectors, :] -= t_dot(panel[:, hi:vectors], panel)
    low = inverse[...]
    for p in range(planes):
        out_ref[pl.ds(p, vectors, stride=planes), :] = dot(low, s_ref[p])


def solve_kernel(inv_ref, low_ref, s_ref, out_ref, upper_ref):
    vectors = inv_ref.shape[0]
    planes = s_ref.shape[0]
    cells = s_ref.shape[2]
    row_i = lax.broadcasted_iota(jnp.int32, (vectors, vectors), 0)
    col_i = lax.broadcasted_iota(jnp.int32, (vectors, vectors), 1)
    upper_ref[...] = jnp.where(col_i >= row_i, low_ref[...].T, 0.0)
    low = inv_ref[...]
    for p in range(0, planes, 2):
        both = dot(low, jnp.concatenate([s_ref[p], s_ref[p + 1]], axis=1))
        out_ref[pl.ds(p, vectors, stride=planes), :] = both[:, 0:cells]
        out_ref[pl.ds(p + 1, vectors, stride=planes), :] = both[:, cells : 2 * cells]


def per_device(tangent, base_state):
    lat_n = lax.axis_size("lat")
    lon_n = lax.axis_size("lon")
    vectors, _, rows, cells = tangent.shape
    planes = 3 * rows
    size = vectors // CHUNKS
    fused = size % (lon_n * 8) == 0
    short = size // lon_n if fused else 8
    f32 = jnp.float32
    x = tangent.reshape(vectors * planes, cells)
    base = base_state.reshape(4 * rows, cells)
    vmem = pl.BlockSpec(memory_space=pltpu.VMEM)
    dma = pltpu.SemaphoreType.DMA
    square = jax.ShapeDtypeStruct((vectors, vectors), f32)
    flat = jax.ShapeDtypeStruct((vectors * planes, cells), f32)
    stepped, first, second = pl.pallas_call(
        functools.partial(step_kernel, lat_n, lon_n, rows, vectors, fused),
        out_shape=(jax.ShapeDtypeStruct((planes, vectors, cells), f32), square, square),
        in_specs=[vmem, vmem],
        out_specs=(vmem, vmem, vmem),
        scratch_shapes=[
            pltpu.VMEM((3, rows, 3, vectors, cells), f32),
            pltpu.VMEM((2, 3, vectors, cells), f32),
            pltpu.VMEM((2, 3, vectors, cells), f32),
            pltpu.VMEM((2, vectors, cells), f32),
            pltpu.VMEM((2, vectors, cells), f32),
            pltpu.VMEM((2, vectors, cells), f32),
            pltpu.VMEM((2, vectors, cells), f32),
            pltpu.VMEM((vectors, vectors), f32),
            pltpu.VMEM((CHUNKS, lon_n - 1, short, vectors), f32),
            pltpu.VMEM((CHUNKS, lat_n, short, vectors), f32),
            pltpu.VMEM((CHUNKS, lon_n, short, vectors), f32),
            dma((2, CHUNKS, 2)), dma((2, CHUNKS, 2)), dma((2, CHUNKS, 2)), dma((2, CHUNKS, 2)),
            dma((CHUNKS, lon_n - 1)), dma((CHUNKS, lon_n - 1)),
            dma((CHUNKS, lat_n - 1)), dma((CHUNKS, lat_n - 1)),
            dma((CHUNKS, lon_n - 1)), dma((CHUNKS, lon_n - 1)),
        ],
        compiler_params=pltpu.CompilerParams(
            collective_id=0, has_side_effects=True, vmem_limit_bytes=40 * 2**20
        ),
    )(x, base)
    local = pltpu.CompilerParams(vmem_limit_bytes=40 * 2**20)
    if fused:
        out, upper = pl.pallas_call(
            solve_kernel,
            out_shape=(flat, square),
            in_specs=[vmem, vmem, vmem],
            out_specs=(vmem, vmem),
            compiler_params=local,
        )(first, second, stepped)
    else:
        total = lax.psum(first, ("lat", "lon"))
        cell_total = rows * cells * lat_n * lon_n
        out, upper = pl.pallas_call(
            functools.partial(factor_kernel, cell_total),
            out_shape=(flat, square),
            in_specs=[vmem, vmem],
            out_specs=(vmem, vmem),
            scratch_shapes=[
                pltpu.VMEM((vectors, 2 * vectors), f32),
                pltpu.VMEM((vectors, vectors), f32),
            ],
            compiler_params=local,
        )(total, stepped)
    return out.reshape(tangent.shape), upper


def solution(mesh):
    in_specs = (P(None, None, "lat", "lon"), P(None, "lat", "lon"))
    out_specs = (P(None, None, "lat", "lon"), P())
    return jax.shard_map(
        per_device, mesh=mesh, in_specs=in_specs, out_specs=out_specs, check_vma=False
    )
```
